32 devices in a mesh: group: 2 (over y), row: 2 (over core), col: 8 (over z, x).
Axes of the slice: x: 2, y: 2, z: 4, core: 2. Of those that a mesh axis runs over, the one named last changes fastest.
Arguments:
- tokens: bfloat16 [1024, 8192], P(('group', 'col'), 'row'), parts along dimension 0, may hold values from -6 to 6
- cotangent: bfloat16 [1024, 8192], P(('group', 'col'), 'row'), parts along dimension 0, may hold values from -6 to 6
- gate_weight: bfloat16 [8192, 16384], P('row', 'col'), may hold values from -0.09375 to 0.09375
- up_weight: bfloat16 [8192, 16384], P('row', 'col'), may hold values from -0.09375 to 0.09375
- down_weight: bfloat16 [16384, 8192], P('col', 'row'), may hold values from -0.0625 to 0.0625
- gate_mask: int32 [64, 128], P('row', 'col'), may hold values from 0 to 1, as said below
- up_mask: int32 [64, 128], P('row', 'col'), may hold values from 0 to 1, as said below
- down_mask: int32 [128, 64], P('col', 'row'), may hold values from 0 to 1, as said below
Outputs:
- output: bfloat16 [1024, 8192], P(('group', 'col'), 'row'), parts along dimension 0
- input_grad: bfloat16 [1024, 8192], P(('group', 'col'), 'row'), parts along dimension 0
- gate_grad: bfloat16 [16384, 16384], P(('group', 'row'), 'col'), parts along dimension 0
- up_grad: bfloat16 [16384, 16384], P(('group', 'row'), 'col'), parts along dimension 0
- down_grad: bfloat16 [32768, 8192], P(('group', 'col'), 'row'), parts along dimension 0
The draws below stay inside these ranges and needn't reach their ends.
There are 2 independent parts, one for each index of `group`. The reference program is written for one: setup_inputs(seed, part) draws one part's arguments, and reference() takes and returns one part's arrays. A program takes and returns all parts, laid end to end along the dimension named above; an argument that names none is the same for every part. Nothing has to cross between parts.
Inputs may be any that keep to these rules, and one draw needn't show every extreme that they name: `gate_mask`: 1 keeps a 128 x 128 block of the projection, 0 removes it. `up_mask`: 1 keeps a 128 x 128 block of the projection, 0 removes it. `down_mask`: 1 keeps a 128 x 128 block of the projection, 0 removes it.
All inputs are finite; a program needn't handle non-finite values.
Results may differ from the reference program's by a relative error of at most 0.005.
Values may be sent and summed in bfloat16 or wider, within the bound.
A program may use at most 320 MiB of HBM per device.

```python
import jax
import jax.numpy as jnp
from jax import lax

D = 8192
FF = 16384
BLOCK = 128
TOKENS = 512


def column_levels(key, shape, salt):
    level_key = jax.random.fold_in(key, salt)
    bit_key = jax.random.fold_in(key, salt + 1)
    levels = jax.random.randint(level_key, (1, shape[1]), 1, 8)
    picks = jax.random.randint(bit_key, shape, 0, 8)
    return (picks < levels).astype(jnp.int32)


def draw_gate_mask(key, part):
    return column_levels(key, (D // BLOCK, FF // BLOCK), 11)


def draw_up_mask(key, part):
    return column_levels(key, (D // BLOCK, FF // BLOCK), 23)


def draw_down_mask(key, part):
    return column_levels(key, (D // BLOCK, FF // BLOCK), 37).T


def block_scale(own_key, extent, shards, low, high):
    def one(position, parts):
        steps = jax.random.uniform(jax.random.fold_in(jax.random.fold_in(own_key, 6), position), (parts,), jnp.float32, low / len(shards), high / len(shards))
        return jnp.repeat(jnp.exp(steps), extent[position] // parts).reshape((-1,) + (1,) * (len(extent) - position - 1))

    factor_of = one(*shards[0])
    for cut in shards[1:]:
        factor_of = factor_of * one(*cut)
    return factor_of


def scatter_about(key, dims, deviation, limit, shards=(), kind=jnp.bfloat16):
    level = block_scale(key, dims, shards, -0.22, 0.18) if shards else 1.0
    values = jax.random.normal(key, dims, jnp.float32) * deviation * level
    return jnp.minimum(jnp.maximum(values, -limit), limit).astype(kind)


def setup_inputs(seed: int = 0, part: int = 0) -> dict:
    key_list = jax.random.split(jax.random.key(seed), 9)
    part_splits = jax.random.split(jax.random.fold_in(key_list[8], part), 9)
    return {
        "tokens": scatter_about(part_splits[0], (TOKENS, D), 1.0, 6.0, ((0, 8), (1, 2))),
        "cotangent": scatter_about(part_splits[1], (TOKENS, D), 1.0, 6.0, ((0, 8), (1, 2))),
        "gate_weight": scatter_about(key_list[2], (D, FF), (D // 2) ** -0.5, 0.09375, ((0, 2), (1, 8))),
        "up_weight": scatter_about(key_list[3], (D, FF), (D // 2) ** -0.5, 0.09375, ((0, 2), (1, 8))),
        "down_weight": scatter_about(key_list[4], (FF, D), (FF // 2) ** -0.5, 0.0625, ((0, 8), (1, 2))),
        "gate_mask": draw_gate_mask(jax.random.fold_in(key_list[8], 71), part),
        "up_mask": draw_up_mask(jax.random.fold_in(key_list[8], 71), part),
        "down_mask": draw_down_mask(jax.random.fold_in(key_list[8], 71), part),
    }


def spread(block_mask):
    expanded = jnp.repeat(jnp.repeat(block_mask, BLOCK, axis=0), BLOCK, axis=1)
    return expanded.astype(jnp.bfloat16)


def contract_rows(left, right):
    return lax.dot_general(left, right, (((0,), (0,)), ((), ())), preferred_element_type=jnp.float32)


def reference(tokens, cotangent, gate_weight, up_weight, down_weight, gate_mask, up_mask, down_mask):
    gate_keep = spread(gate_mask)
    up_keep = spread(up_mask)
    down_keep = spread(down_mask)
    gate_eff = gate_weight * gate_keep
    up_eff = up_weight * up_keep
    down_eff = down_weight * down_keep
    gate_pre = jnp.dot(tokens, gate_eff, preferred_element_type=jnp.float32)
    up_pre = jnp.dot(tokens, up_eff, preferred_element_type=jnp.float32)
    sigmoid_gate = jax.nn.sigmoid(gate_pre)
    activated = gate_pre * sigmoid_gate
    hidden = (activated * up_pre).astype(jnp.bfloat16)
    output = jnp.dot(hidden, down_eff, preferred_element_type=jnp.float32).astype(jnp.bfloat16)
    hidden_grad = jnp.dot(cotangent, down_eff.T, preferred_element_type=jnp.float32)
    gate_delta = (hidden_grad * up_pre * sigmoid_gate * (1.0 + gate_pre * (1.0 - sigmoid_gate))).astype(jnp.bfloat16)
    up_delta = (hidden_grad * activated).astype(jnp.bfloat16)
    input_grad = (jnp.dot(gate_delta, gate_eff.T, preferred_element_type=jnp.float32)
                  + jnp.dot(up_delta, up_eff.T, preferred_element_type=jnp.float32)).astype(jnp.bfloat16)
    gate_grad = (contract_rows(tokens, gate_delta) * gate_keep).astype(jnp.bfloat16)
    up_grad = (contract_rows(tokens, up_delta) * up_keep).astype(jnp.bfloat16)
    down_grad = (contract_rows(hidden, cotangent) * down_keep).astype(jnp.bfloat16)
    return (output, input_grad, gate_grad, up_grad, down_grad)
```

```python
import functools

import jax
import jax.numpy as jnp
from jax import lax
from jax.experimental import pallas as pl
from jax.experimental.pallas import tpu as pltpu
from jax.sharding import PartitionSpec as P

BLOCK = 128
TILE = 256
VMEM_LIMIT = 52 * 1024 * 1024
F32, BF16 = jnp.float32, jnp.bfloat16

WALK = (0, 2, 4, 6, 7, 5, 3, 1)
FORWARD = [(WALK[i], WALK[(i + 1) % 8]) for i in range(8)]
BACKWARD = [(b, a) for a, b in FORWARD]


def dot(left, right, dims):
    return lax.dot_general(left, right, (dims, ((), ())), preferred_element_type=F32)


def keep_rows(flag):
    return jnp.full((1, BLOCK), flag, jnp.int32).astype(F32)


def masked_into(dst, weight, mask, row0, col0):
    for r in range(weight.shape[0] // BLOCK):
        for c in range(weight.shape[1] // BLOCK):
            rows, cols = pl.ds(r * BLOCK, BLOCK), pl.ds(c * BLOCK, BLOCK)
            keep = keep_rows(mask[row0 + r, col0 + c]).astype(BF16)
            dst[rows, cols] = weight[rows, cols] * keep


def call(kernel, grid, ins, in_specs, outs, out_specs, scratch, flops):
    moved = sum(a.size * a.dtype.itemsize for a in [*ins, *outs])
    return pl.pallas_call(
        kernel,
        grid=(grid,),
        in_specs=in_specs,
        out_specs=out_specs,
        out_shape=outs,
        scratch_shapes=scratch,
        compiler_params=pltpu.CompilerParams(vmem_limit_bytes=VMEM_LIMIT),
        cost_estimate=pl.CostEstimate(flops=flops, bytes_accessed=moved, transcendentals=0),
    )(*ins)


def whole(shape):
    return pl.BlockSpec(shape, lambda i: (0, 0))


def by_cols(rows, width):
    return pl.BlockSpec((rows, width), lambda i: (0, i))


def by_rows(height, cols):
    return pl.BlockSpec((height, cols), lambda i: (i, 0))


SMEM = pl.BlockSpec(memory_space=pltpu.SMEM)


def pre_kernel(t, gw, uw, gm, um, g32, u32, g16, u16, ge, ue):
    col0 = pl.program_id(0) * (TILE // BLOCK)
    for w, m, eff, full, short in ((gw, gm, ge, g32, g16), (uw, um, ue, u32, u16)):
        masked_into(eff, w, m, 0, col0)
        total = dot(t[...], eff[...], ((1,), (0,)))
        full[...] = total
        short[...] = total.astype(BF16)


def pre_activations(t, gw, uw, gm, um):
    m, k = t.shape
    n = gw.shape[1]
    outs = [jax.ShapeDtypeStruct((m, n), d) for d in (F32, F32, BF16, BF16)]
    return call(
        pre_kernel, n // TILE, [t, gw, uw, gm, um],
        [whole((m, k)), by_cols(k, TILE), by_cols(k, TILE), SMEM, SMEM],
        outs, [by_cols(m, TILE)] * 4, [pltpu.VMEM((k, TILE), BF16)] * 2, 4 * m * k * n,
    )


def hgrad_kernel(c, dw, dm, full, short, eff):
    masked_into(eff, dw, dm, pl.program_id(0) * (TILE // BLOCK), 0)
    total = dot(c[...], eff[...], ((1,), (1,)))
    full[...] = total
    short[...] = total.astype(BF16)


def hidden_gradient(c, dw, dm):
    m, k = c.shape
    n = dw.shape[0]
    outs = [jax.ShapeDtypeStruct((m, n), d) for d in (F32, BF16)]
    return call(
        hgrad_kernel, n // TILE, [c, dw, dm], [whole((m, k)), by_rows(TILE, k), SMEM],
        outs, [by_cols(m, TILE)] * 2, [pltpu.VMEM((TILE, k), BF16)], 2 * m * k * n,
    )


def out_kernel(h, dw, dm, out, eff):
    masked_into(eff, dw, dm, 0, pl.program_id(0) * (eff.shape[1] // BLOCK))
    out[...] = dot(h[...], eff[...], ((1,), (0,))).astype(out.dtype)


def output_partial(h, dw, dm, dtype):
    m, k = h.shape
    n = dw.shape[1]
    tile = 2 * TILE
    return call(
        out_kernel, n // tile, [h, dw, dm], [whole((m, k)), by_cols(k, tile), SMEM],
        [jax.ShapeDtypeStruct((m, n), dtype)], [by_cols(m, tile)],
        [pltpu.VMEM((k, tile), BF16)], 2 * m * k * n,
    )[0]


def in_kernel(gd, ud, gw, uw, gm, um, out, ge, ue):
    row0 = pl.program_id(0) * (ge.shape[0] // BLOCK)
    masked_into(ge, gw, gm, row0, 0)
    masked_into(ue, uw, um, row0, 0)
    dims = ((1,), (1,))
    out[...] = (dot(gd[...], ge[...], dims) + dot(ud[...], ue[...], dims)).astype(out.dtype)


def input_partial(gd, ud, gw, uw, gm, um, dtype):
    m, k = gd.shape
    n = gw.shape[0]
    tile = 2 * TILE
    return call(
        in_kernel, n // tile, [gd, ud, gw, uw, gm, um],
        [whole((m, k))] * 2 + [by_rows(tile, k)] * 2 + [SMEM] * 2,
        [jax.ShapeDtypeStruct((m, n), dtype)], [by_cols(m, tile)],
        [pltpu.VMEM((tile, k), BF16)] * 2, 4 * m * k * n,
    )[0]


def grads_kernel(count, *refs):
    left = refs[0]
    rights, masks, outs = refs[1:1 + count], refs[1 + count:1 + 2 * count], refs[1 + 2 * count:]
    flipped = left[...].T
    row0 = pl.program_id(0) * (left.shape[1] // BLOCK)
    for right, mask, out in zip(rights, masks, outs):
        for col in range(0, right.shape[1], TILE):
            total = dot(flipped, right[:, col:col + TILE], ((1,), (0,)))
            for r in range(left.shape[1] // BLOCK):
                for c in range(TILE // BLOCK):
                    keep = keep_rows(mask[row0 + r, col // BLOCK + c])
                    part = total[r * BLOCK:(r + 1) * BLOCK, c * BLOCK:(c + 1) * BLOCK]
                    out[pl.ds(r * BLOCK, BLOCK), pl.ds(col + c * BLOCK, BLOCK)] = (part * keep).astype(BF16)


def weight_grads(left, rights, masks):
    m, k = left.shape
    n = rights[0].shape[1]
    tile = min(2 * TILE, k)
    count = len(rights)
    return call(
        functools.partial(grads_kernel, count), k // tile, [left, *rights, *masks],
        [by_cols(m, tile)] + [whole((m, n))] * count + [SMEM] * count,
        [jax.ShapeDtypeStruct((k, n), BF16)] * count, [by_rows(tile, n)] * count, [], 2 * m * k * n * count,
    )


def ring_gather(x):
    half = x.shape[0] // 2
    ahead, behind = [x], [x]
    for _ in range(3):
        behind.append(lax.ppermute(behind[-1], "col", FORWARD))
        ahead.append(lax.ppermute(ahead[-1], "col", BACKWARD))
    top = lax.ppermute(behind[-1][:half], "col", FORWARD)
    bottom = lax.ppermute(ahead[-1][half:], "col", BACKWARD)
    return jnp.concatenate([*ahead, top, bottom, *behind[:0:-1]], axis=0)


def add(a, b):
    return (a.astype(F32) + b.astype(F32)).astype(BF16)


def ring_scatter(partial):
    rows = partial.shape[0] // 8
    half = partial.shape[1] // 2
    part = [partial[j * rows:(j + 1) * rows] for j in range(8)]
    first = lax.ppermute(part[4][:, :half], "col", FORWARD)
    second = lax.ppermute(part[4][:, half:], "col", BACKWARD)
    forward = jnp.concatenate([add(part[3][:, :half], first), part[3][:, half:]], axis=1)
    backward = jnp.concatenate([part[5][:, :half], add(part[5][:, half:], second)], axis=1)
    for step in range(2):
        forward = add(part[2 - step], lax.ppermute(forward, "col", FORWARD))
        backward = add(part[6 + step], lax.ppermute(backward, "col", BACKWARD))
    forward = lax.ppermute(forward, "col", FORWARD)
    backward = lax.ppermute(backward, "col", BACKWARD)
    return (part[0].astype(F32) + forward.astype(F32) + backward.astype(F32)).astype(BF16)


def plain_gather(x):
    return lax.all_gather(x, "col", axis=0, tiled=True)


def plain_scatter(partial):
    return lax.psum_scatter(partial, "col", scatter_dimension=0, tiled=True).astype(BF16)


def body(ring, tokens, cotangent, gate_weight, up_weight, down_weight, gate_mask, up_mask, down_mask):
    gather, scatter = (ring_gather, ring_scatter) if ring else (plain_gather, plain_scatter)
    sent = BF16 if ring else F32

    def other_row(x):
        return lax.ppermute(x, "row", [(0, 1), (1, 0)]).astype(F32)

    features = gather(tokens)
    features, cotangent = lax.optimization_barrier((features, cotangent))
    shard_rows = gather(cotangent)
    gate_own, up_own, gate_sent, up_sent = pre_activations(features, gate_weight, up_weight, gate_mask, up_mask)
    gate_pre = gate_own + other_row(gate_sent)
    up_pre = up_own + other_row(up_sent)
    sigmoid_gate = jax.nn.sigmoid(gate_pre)
    activated = gate_pre * sigmoid_gate
    hidden = (activated * up_pre).astype(BF16)
    output = scatter(output_partial(hidden, down_weight, down_mask, sent))
    grad_own, grad_sent = hidden_gradient(shard_rows, down_weight, down_mask)
    hidden_grad = grad_own + other_row(grad_sent)
    gate_delta = (hidden_grad * up_pre * sigmoid_gate * (1.0 + gate_pre * (1.0 - sigmoid_gate))).astype(BF16)
    up_delta = (hidden_grad * activated).astype(BF16)
    input_grad = scatter(input_partial(gate_delta, up_delta, gate_weight, up_weight, gate_mask, up_mask, sent))
    gate_grad, up_grad = weight_grads(features, [gate_delta, up_delta], [gate_mask, up_mask])
    (down_grad,) = weight_grads(hidden, [shard_rows], [down_mask])
    return (output, input_grad, gate_grad, up_grad, down_grad)


def solution(mesh):
    in_specs = (
        P(("group", "col"), "row"),
        P(("group", "col"), "row"),
        P("row", "col"),
        P("row", "col"),
        P("col", "row"),
        P("row", "col"),
        P("row", "col"),
        P("col", "row"),
    )
    out_specs = (
        P(("group", "col"), "row"),
        P(("group", "col"), "row"),
        P(("group", "row"), "col"),
        P(("group", "row"), "col"),
        P(("group", "col"), "row"),
    )
    step = functools.partial(body, mesh.shape["col"] == 8)
    return jax.shard_map(step, mesh=mesh, in_specs=in_specs, out_specs=out_specs, check_vma=False)
```

```python
import functools

import jax
import jax.numpy as jnp
from jax import lax
from jax.experimental import pallas as pl
from jax.experimental.pallas import tpu as pltpu
from jax.sharding import PartitionSpec as P

BLOCK = 128
TILE = 256
VMEM_LIMIT = 52 * 1024 * 1024
F32, BF16 = jnp.float32, jnp.bfloat16

WALK = (0, 2, 4, 6, 7, 5, 3, 1)
FORWARD = [(WALK[i], WALK[(i + 1) % 8]) for i in range(8)]
BACKWARD = [(b, a) for a, b in FORWARD]


def dot(left, right, dims):
    return lax.dot_general(left, right, (dims, ((), ())), preferred_element_type=F32)


def keep_rows(flag):
    return jnp.full((1, BLOCK), flag, jnp.int32).astype(F32)


def masked_into(dst, weight, mask, row0, col0):
    for r in range(weight.shape[0] // BLOCK):
        for c in range(weight.shape[1] // BLOCK):
            rows, cols = pl.ds(r * BLOCK, BLOCK), pl.ds(c * BLOCK, BLOCK)
            keep = keep_rows(mask[row0 + r, col0 + c]).astype(BF16)
            dst[rows, cols] = weight[rows, cols] * keep


def call(kernel, grid, ins, in_specs, outs, out_specs, scratch, flops, after=(), into=None):
    extra = list(after) + ([] if into is None else [into])
    used, unused = len(ins), len(extra)

    def run(*refs):
        kernel(*refs[:used], *refs[used + unused:])

    moved = sum(a.size * a.dtype.itemsize for a in [*ins, *outs])
    return pl.pallas_call(
        run,
        grid=(grid,),
        in_specs=[*in_specs] + [pl.BlockSpec(memory_space=pl.ANY)] * unused,
        out_specs=out_specs,
        out_shape=outs,
        scratch_shapes=scratch,
        input_output_aliases={} if into is None else {used + unused - 1: 0},
        compiler_params=pltpu.CompilerParams(vmem_limit_bytes=VMEM_LIMIT),
        cost_estimate=pl.CostEstimate(flops=flops, bytes_accessed=moved, transcendentals=0),
    )(*ins, *extra)


def whole(shape):
    return pl.BlockSpec(shape, lambda i: (0, 0))


def by_cols(rows, width, first=0):
    return pl.BlockSpec((rows, width), lambda i: (0, i + first))


def by_rows(height, cols, first=0):
    return pl.BlockSpec((height, cols), lambda i: (i + first, 0))


SMEM = pl.BlockSpec(memory_space=pltpu.SMEM)


def pre_kernel(t, w, m, full, short, eff):
    masked_into(eff, w, m, 0, pl.program_id(0) * (TILE // BLOCK))
    total = dot(t[...], eff[...], ((1,), (0,)))
    full[...] = total
    short[...] = total.astype(BF16)


def pre_activation(t, w, mask, after=()):
    m, k = t.shape
    n = w.shape[1]
    outs = [jax.ShapeDtypeStruct((m, n), d) for d in (F32, BF16)]
    return call(
        pre_kernel, n // TILE, [t, w, mask], [whole((m, k)), by_cols(k, TILE), SMEM],
        outs, [by_cols(m, TILE)] * 2, [pltpu.VMEM((k, TILE), BF16)], 2 * m * k * n, after,
    )


def hgrad_kernel(first, c, dw, dm, out, eff):
    masked_into(eff, dw, dm, (pl.program_id(0) + first) * (TILE // BLOCK), 0)
    out[...] = dot(c[...], eff[...], ((1,), (1,)))


def hidden_gradient(c, dw, dm, first, tiles, after=()):
    m, k = c.shape
    return call(
        functools.partial(hgrad_kernel, first), tiles, [c, dw, dm],
        [whole((m, k)), by_rows(TILE, k, first), SMEM],
        [jax.ShapeDtypeStruct((m, tiles * TILE), F32)], [by_cols(m, TILE)],
        [pltpu.VMEM((TILE, k), BF16)], 2 * m * k * tiles * TILE, after,
    )[0]


def out_kernel(first, h, dw, dm, out, eff):
    masked_into(eff, dw, dm, 0, (pl.program_id(0) + first) * (eff.shape[1] // BLOCK))
    out[...] = dot(h[...], eff[...], ((1,), (0,)))


def output_partial(h, dw, dm, first, tiles, after=()):
    m, k = h.shape
    tile = 2 * TILE
    return call(
        functools.partial(out_kernel, first), tiles, [h, dw, dm],
        [whole((m, k)), by_cols(k, tile, first), SMEM],
        [jax.ShapeDtypeStruct((m, tiles * tile), F32)], [by_cols(m, tile)],
        [pltpu.VMEM((k, tile), BF16)], 2 * m * k * tiles * tile, after,
    )[0]


def in_kernel(first, gd, ud, gw, uw, gm, um, out, ge, ue):
    row0 = (pl.program_id(0) + first) * (ge.shape[0] // BLOCK)
    masked_into(ge, gw, gm, row0, 0)
    masked_into(ue, uw, um, row0, 0)
    dims = ((1,), (1,))
    out[...] = dot(gd[...], ge[...], dims) + dot(ud[...], ue[...], dims)


def input_partial(gd, ud, gw, uw, gm, um, first, tiles, after=()):
    m, k = gd.shape
    tile = 2 * TILE
    return call(
        functools.partial(in_kernel, first), tiles, [gd, ud, gw, uw, gm, um],
        [whole((m, k))] * 2 + [by_rows(tile, k, first)] * 2 + [SMEM] * 2,
        [jax.ShapeDtypeStruct((m, tiles * tile), F32)], [by_cols(m, tile)],
        [pltpu.VMEM((tile, k), BF16)] * 2, 4 * m * k * tiles * tile, after,
    )[0]


def grads_kernel(first, left, right, mask, out):
    flipped = left[...].T
    row0 = (pl.program_id(0) + first) * (left.shape[1] // BLOCK)
    for col in range(0, right.shape[1], TILE):
        total = dot(flipped, right[:, col:col + TILE], ((1,), (0,)))
        for r in range(left.shape[1] // BLOCK):
            for c in range(TILE // BLOCK):
                keep = keep_rows(mask[row0 + r, col // BLOCK + c])
                part = total[r * BLOCK:(r + 1) * BLOCK, c * BLOCK:(c + 1) * BLOCK]
                out[pl.ds(r * BLOCK, BLOCK), pl.ds(col + c * BLOCK, BLOCK)] = (part * keep).astype(BF16)


def weight_grad(left, right, mask, after=(), share=(0, 1), into=None):
    m, k = left.shape
    n = right.shape[1]
    tile = min(2 * TILE, k)
    first = share[0] * (k // tile) // 2 if share[1] == 2 else 0
    last = (share[0] + 1) * (k // tile) // 2 if share[1] == 2 else k // tile
    return call(
        functools.partial(grads_kernel, first), last - first, [left, right, mask],
        [by_cols(m, tile, first), whole((m, n)), SMEM],
        [jax.ShapeDtypeStruct((k, n), BF16)], [by_rows(tile, n, first)], [],
        2 * m * (last - first) * tile * n, after, into,
    )[0]


def ring_gather(x, arrived):
    half = x.shape[0] // 2
    ahead, behind = [x], [x]
    for _ in range(3):
        behind.append(lax.ppermute(behind[-1], "col", FORWARD))
        ahead.append(lax.ppermute(ahead[-1], "col", BACKWARD))
        arrived.append((behind[-1], ahead[-1]))
    top = lax.ppermute(behind[-1][:half], "col", FORWARD)
    bottom = lax.ppermute(ahead[-1][half:], "col", BACKWARD)
    return jnp.concatenate([*ahead, top, bottom, *behind[:0:-1]], axis=0)


def plain_gather(x, arrived):
    arrived.extend([()] * 3)
    return lax.all_gather(x, "col", axis=0, tiled=True)


def ring_scatter(left, right):
    rows = left.shape[0] // 8

    def own(j):
        return left[j * rows:(j + 1) * rows], right[j * rows:(j + 1) * rows]

    sent = own(4)[0].astype(BF16), own(4)[1].astype(BF16)
    yield sent
    first, second = lax.ppermute(sent[0], "col", FORWARD), lax.ppermute(sent[1], "col", BACKWARD)
    forward = jnp.concatenate([own(3)[0] + first.astype(F32), own(3)[1]], axis=1).astype(BF16)
    backward = jnp.concatenate([own(5)[0], own(5)[1] + second.astype(F32)], axis=1).astype(BF16)
    yield forward, backward
    for step in range(2):
        mine, theirs = jnp.concatenate(own(2 - step), axis=1), jnp.concatenate(own(6 + step), axis=1)
        forward = (mine + lax.ppermute(forward, "col", FORWARD).astype(F32)).astype(BF16)
        backward = (theirs + lax.ppermute(backward, "col", BACKWARD).astype(F32)).astype(BF16)
        yield forward, backward
    forward = lax.ppermute(forward, "col", FORWARD).astype(F32)
    backward = lax.ppermute(backward, "col", BACKWARD).astype(F32)
    yield (jnp.concatenate(own(0), axis=1) + forward + backward).astype(BF16)


def plain_scatter(left, right):
    for _ in range(4):
        yield ()
    partial = jnp.concatenate([left, right], axis=1)
    yield lax.psum_scatter(partial, "col", scatter_dimension=0, tiled=True).astype(BF16)


def body(ring, tokens, cotangent, gate_weight, up_weight, down_weight, gate_mask, up_mask, down_mask):
    gather, scatter = (ring_gather, ring_scatter) if ring else (plain_gather, plain_scatter)

    def other_row(x):
        return lax.ppermute(x, "row", [(0, 1), (1, 0)]).astype(F32)

    features = gather(tokens, [])
    features, cotangent = lax.optimization_barrier((features, cotangent))
    arrived = []
    shard_rows = gather(cotangent, arrived)
    gate_own, gate_sent = pre_activation(features, gate_weight, gate_mask)
    up_own, up_sent = pre_activation(features, up_weight, up_mask, [gate_sent, *arrived[0]])
    gate_pre = gate_own + other_row(gate_sent)
    up_pre = up_own + other_row(up_sent)
    sigmoid_gate = jax.nn.sigmoid(gate_pre)
    activated = gate_pre * sigmoid_gate
    hidden = (activated * up_pre).astype(BF16)

    halves = tokens.shape[1] // (4 * TILE)
    left = output_partial(hidden, down_weight, down_mask, 0, halves, arrived[1])
    right = output_partial(hidden, down_weight, down_mask, halves, halves, [left, *arrived[2]])
    out_steps = scatter(left, right)

    tiles = hidden.shape[1] // TILE
    cuts = [(0, tiles // 2), (tiles // 2, tiles - tiles // 2)] if tiles > 1 else [(0, 1)]
    grads = []
    for first, count in cuts:
        own = hidden_gradient(shard_rows, down_weight, down_mask, first, count, next(out_steps))
        grads.append(own + other_row(own))
    for _ in range(2 - len(cuts)):
        next(out_steps)
    hidden_grad = jnp.concatenate(grads, axis=1)
    gate_delta = (hidden_grad * up_pre * sigmoid_gate * (1.0 + gate_pre * (1.0 - sigmoid_gate))).astype(BF16)
    up_delta = (hidden_grad * activated).astype(BF16)
    weights = gate_delta, up_delta, gate_weight, up_weight, gate_mask, up_mask
    left = input_partial(*weights, 0, halves, next(out_steps))
    right = input_partial(*weights, halves, halves, [left, *next(out_steps)])
    output = next(out_steps)

    in_steps = scatter(left, right)
    split = hidden.shape[1] > 2 * TILE
    down_grad = weight_grad(
        hidden, shard_rows, down_mask, [left, right, *next(in_steps)], (0, 2) if split else (0, 1)
    )
    gate_grad = weight_grad(features, gate_delta, gate_mask, next(in_steps))
    up_grad = weight_grad(features, up_delta, up_mask, next(in_steps))
    last = next(in_steps)
    if split:
        down_grad = weight_grad(hidden, shard_rows, down_mask, last, (1, 2), down_grad)
    input_grad = next(in_steps)
    return (output, input_grad, gate_grad, up_grad, down_grad)


def solution(mesh):
    in_specs = (
        P(("group", "col"), "row"),
        P(("group", "col"), "row"),
        P("row", "col"),
        P("row", "col"),
        P("col", "row"),
        P("row", "col"),
        P("row", "col"),
        P("col", "row"),
    )
    out_specs = (
        P(("group", "col"), "row"),
        P(("group", "col"), "row"),
        P(("group", "row"), "col"),
        P(("group", "row"), "col"),
        P(("group", "col"), "row"),
    )
    step = functools.partial(body, mesh.shape["col"] == 8)
    return jax.shard_map(step, mesh=mesh, in_specs=in_specs, out_specs=out_specs, check_vma=False)
```

```python
import functools

import jax
import jax.numpy as jnp
from jax import lax
from jax.experimental import pallas as pl
from jax.experimental.pallas import tpu as pltpu
from jax.sharding import PartitionSpec as P

BLOCK = 128
TILE = 256
VMEM_LIMIT = 52 * 1024 * 1024
F32, BF16 = jnp.float32, jnp.bfloat16

WALK = (0, 2, 4, 6, 7, 5, 3, 1)
FORWARD = [(WALK[i], WALK[(i + 1) % 8]) for i in range(8)]
BACKWARD = [(b, a) for a, b in FORWARD]


def dot(left, right, dims):
    return lax.dot_general(left, right, (dims, ((), ())), preferred_element_type=F32)


def keep_rows(flag):
    return jnp.full((1, BLOCK), flag, jnp.int32).astype(F32)


def masked_into(dst, weight, mask, row0, col0):
    for r in range(weight.shape[0] // BLOCK):
        for c in range(weight.shape[1] // BLOCK):
            rows, cols = pl.ds(r * BLOCK, BLOCK), pl.ds(c * BLOCK, BLOCK)
            keep = keep_rows(mask[row0 + r, col0 + c]).astype(BF16)
            dst[rows, cols] = weight[rows, cols] * keep


def call(kernel, grid, ins, in_specs, outs, out_specs, scratch, flops, after=(), into=None):
    extra = list(after) + ([] if into is None else [into])
    used, unused = len(ins), len(extra)

    def run(*refs):
        kernel(*refs[:used], *refs[used + unused:])

    moved = sum(a.size * a.dtype.itemsize for a in [*ins, *outs])
    return pl.pallas_call(
        run,
        grid=(grid,),
        in_specs=[*in_specs] + [pl.BlockSpec(memory_space=pl.ANY)] * unused,
        out_specs=out_specs,
        out_shape=outs,
        scratch_shapes=scratch,
        input_output_aliases={} if into is None else {used + unused - 1: 0},
        compiler_params=pltpu.CompilerParams(vmem_limit_bytes=VMEM_LIMIT),
        cost_estimate=pl.CostEstimate(flops=flops, bytes_accessed=moved, transcendentals=0),
    )(*ins, *extra)


def whole(shape):
    return pl.BlockSpec(shape, lambda i: (0, 0))


def by_cols(rows, width, first=0):
    return pl.BlockSpec((rows, width), lambda i: (0, i + first))


def by_rows(height, cols, first=0):
    return pl.BlockSpec((height, cols), lambda i: (i + first, 0))


SMEM = pl.BlockSpec(memory_space=pltpu.SMEM)


def pre_kernel(t, w, m, full, short, eff):
    masked_into(eff, w, m, 0, pl.program_id(0) * (TILE // BLOCK))
    total = dot(t[...], eff[...], ((1,), (0,)))
    full[...] = total
    short[...] = total.astype(BF16)


def pre_activation(t, w, mask, after=()):
    m, k = t.shape
    n = w.shape[1]
    outs = [jax.ShapeDtypeStruct((m, n), d) for d in (F32, BF16)]
    return call(
        pre_kernel, n // TILE, [t, w, mask], [whole((m, k)), by_cols(k, TILE), SMEM],
        outs, [by_cols(m, TILE)] * 2, [pltpu.VMEM((k, TILE), BF16)], 2 * m * k * n, after,
    )


def hgrad_kernel(first, c, dw, dm, out, eff):
    masked_into(eff, dw, dm, (pl.program_id(0) + first) * (TILE // BLOCK), 0)
    out[...] = dot(c[...], eff[...], ((1,), (1,)))


def hidden_gradient(c, dw, dm, first, tiles, after=()):
    m, k = c.shape
    return call(
        functools.partial(hgrad_kernel, first), tiles, [c, dw, dm],
        [whole((m, k)), by_rows(TILE, k, first), SMEM],
        [jax.ShapeDtypeStruct((m, tiles * TILE), F32)], [by_cols(m, TILE)],
        [pltpu.VMEM((TILE, k), BF16)], 2 * m * k * tiles * TILE, after,
    )[0]


def out_kernel(first, h, dw, dm, out, eff):
    masked_into(eff, dw, dm, 0, (pl.program_id(0) + first) * (eff.shape[1] // BLOCK))
    out[...] = dot(h[...], eff[...], ((1,), (0,)))


def output_partial(h, dw, dm, first, tiles, after=()):
    m, k = h.shape
    tile = 2 * TILE
    return call(
        functools.partial(out_kernel, first), tiles, [h, dw, dm],
        [whole((m, k)), by_cols(k, tile, first), SMEM],
        [jax.ShapeDtypeStruct((m, tiles * tile), F32)], [by_cols(m, tile)],
        [pltpu.VMEM((k, tile), BF16)], 2 * m * k * tiles * tile, after,
    )[0]


def in_kernel(first, gd, ud, gw, uw, gm, um, out, ge, ue):
    row0 = (pl.program_id(0) + first) * (ge.shape[0] // BLOCK)
    masked_into(ge, gw, gm, row0, 0)
    masked_into(ue, uw, um, row0, 0)
    dims = ((1,), (1,))
    out[...] = dot(gd[...], ge[...], dims) + dot(ud[...], ue[...], dims)


def input_partial(gd, ud, gw, uw, gm, um, first, tiles, after=()):
    m, k = gd.shape
    tile = 2 * TILE
    return call(
        functools.partial(in_kernel, first), tiles, [gd, ud, gw, uw, gm, um],
        [whole((m, k))] * 2 + [by_rows(tile, k, first)] * 2 + [SMEM] * 2,
        [jax.ShapeDtypeStruct((m, tiles * tile), F32)], [by_cols(m, tile)],
        [pltpu.VMEM((tile, k), BF16)] * 2, 4 * m * k * tiles * tile, after,
    )[0]


def grads_kernel(first, left, right, mask, out):
    flipped = left[...].T
    row0 = (pl.program_id(0) + first) * (left.shape[1] // BLOCK)
    for col in range(0, right.shape[1], TILE):
        total = dot(flipped, right[:, col:col + TILE], ((1,), (0,)))
        for r in range(left.shape[1] // BLOCK):
            for c in range(TILE // BLOCK):
                keep = keep_rows(mask[row0 + r, col // BLOCK + c])
                part = total[r * BLOCK:(r + 1) * BLOCK, c * BLOCK:(c + 1) * BLOCK]
                out[pl.ds(r * BLOCK, BLOCK), pl.ds(col + c * BLOCK, BLOCK)] = (part * keep).astype(BF16)


def weight_grad(left, right, mask, after=(), share=(0, 1), into=None):
    m, k = left.shape
    n = right.shape[1]
    tile = min(2 * TILE, k)
    first = share[0] * (k // tile) // 2 if share[1] == 2 else 0
    last = (share[0] + 1) * (k // tile) // 2 if share[1] == 2 else k // tile
    return call(
        functools.partial(grads_kernel, first), last - first, [left, right, mask],
        [by_cols(m, tile, first), whole((m, n)), SMEM],
        [jax.ShapeDtypeStruct((k, n), BF16)], [by_rows(tile, n, first)], [],
        2 * m * (last - first) * tile * n, after, into,
    )[0]


def ring_gather(x, arrived):
    half = x.shape[0] // 2
    ahead, behind = [x], [x]
    for _ in range(3):
        behind.append(lax.ppermute(behind[-1], "col", FORWARD))
        ahead.append(lax.ppermute(ahead[-1], "col", BACKWARD))
        arrived.append((behind[-1], ahead[-1]))
    top = lax.ppermute(behind[-1][:half], "col", FORWARD)
    bottom = lax.ppermute(ahead[-1][half:], "col", BACKWARD)
    return jnp.concatenate([*ahead, top, bottom, *behind[:0:-1]], axis=0)


def plain_gather(x, arrived):
    arrived.extend([()] * 3)
    return lax.all_gather(x, "col", axis=0, tiled=True)


def ring_scatter(left, right):
    rows = left.shape[0] // 8

    def own(j):
        return left[j * rows:(j + 1) * rows], right[j * rows:(j + 1) * rows]

    low, high = lax.optimization_barrier(own(4))
    sent = low.astype(BF16), high.astype(BF16)
    yield sent
    first, second = lax.ppermute(sent[0], "col", FORWARD), lax.ppermute(sent[1], "col", BACKWARD)
    forward = jnp.concatenate([own(3)[0] + first.astype(F32), own(3)[1]], axis=1).astype(BF16)
    backward = jnp.concatenate([own(5)[0], own(5)[1] + second.astype(F32)], axis=1).astype(BF16)
    yield forward, backward
    for step in range(2):
        mine, theirs = jnp.concatenate(own(2 - step), axis=1), jnp.concatenate(own(6 + step), axis=1)
        forward = (mine + lax.ppermute(forward, "col", FORWARD).astype(F32)).astype(BF16)
        backward = (theirs + lax.ppermute(backward, "col", BACKWARD).astype(F32)).astype(BF16)
        gate = yield forward, backward
        if gate is not None:
            forward, backward, _ = lax.optimization_barrier((forward, backward, gate))
    forward = lax.ppermute(forward, "col", FORWARD).astype(F32)
    backward = lax.ppermute(backward, "col", BACKWARD).astype(F32)
    yield (jnp.concatenate(own(0), axis=1) + forward + backward).astype(BF16)


def plain_scatter(left, right):
    for _ in range(4):
        yield ()
    partial = jnp.concatenate([left, right], axis=1)
    yield lax.psum_scatter(partial, "col", scatter_dimension=0, tiled=True).astype(BF16)


def body(ring, tokens, cotangent, gate_weight, up_weight, down_weight, gate_mask, up_mask, down_mask):
    gather, scatter = (ring_gather, ring_scatter) if ring else (plain_gather, plain_scatter)

    def other_row(x):
        return lax.ppermute(x, "row", [(0, 1), (1, 0)]).astype(F32)

    features = gather(tokens, [])
    features, cotangent = lax.optimization_barrier((features, cotangent))
    arrived = []
    shard_rows = gather(cotangent, arrived)
    gate_own, gate_sent = pre_activation(features, gate_weight, gate_mask)
    up_own, up_sent = pre_activation(features, up_weight, up_mask, [gate_sent, *arrived[0]])
    gate_pre = gate_own + other_row(gate_sent)
    up_pre = up_own + other_row(up_sent)
    sigmoid_gate = jax.nn.sigmoid(gate_pre)
    activated = gate_pre * sigmoid_gate
    hidden = (activated * up_pre).astype(BF16)

    halves = tokens.shape[1] // (4 * TILE)
    left = output_partial(hidden, down_weight, down_mask, 0, halves, arrived[1])
    right = output_partial(hidden, down_weight, down_mask, halves, halves, [left, *arrived[2]])
    out_steps = scatter(left, right)

    tiles = hidden.shape[1] // TILE
    cuts = [(0, tiles // 2), (tiles // 2, tiles - tiles // 2)] if tiles > 1 else [(0, 1)]
    grads = []
    for first, count in cuts:
        own = hidden_gradient(shard_rows, down_weight, down_mask, first, count, next(out_steps))
        grads.append(own + other_row(own))
    for _ in range(2 - len(cuts)):
        next(out_steps)
    hidden_grad = jnp.concatenate(grads, axis=1)
    gate_delta = (hidden_grad * up_pre * sigmoid_gate * (1.0 + gate_pre * (1.0 - sigmoid_gate))).astype(BF16)
    up_delta = (hidden_grad * activated).astype(BF16)
    weights = gate_delta, up_delta, gate_weight, up_weight, gate_mask, up_mask
    next(out_steps)
    left = input_partial(*weights, 0, halves)
    right = input_partial(*weights, halves, halves, [left, *out_steps.send(gate_delta)])
    output = next(out_steps)

    in_steps = scatter(left, right)
    split = hidden.shape[1] > 2 * TILE
    down_grad = weight_grad(
        hidden, shard_rows, down_mask, [left, right, *next(in_steps)], (0, 2) if split else (0, 1)
    )
    gate_grad = weight_grad(features, gate_delta, gate_mask, next(in_steps))
    up_grad = weight_grad(features, up_delta, up_mask, next(in_steps))
    last = next(in_steps)
    if split:
        down_grad = weight_grad(hidden, shard_rows, down_mask, last, (1, 2), down_grad)
    input_grad = next(in_steps)
    return (output, input_grad, gate_grad, up_grad, down_grad)


def solution(mesh):
    in_specs = (
        P(("group", "col"), "row"),
        P(("group", "col"), "row"),
        P("row", "col"),
        P("row", "col"),
        P("col", "row"),
        P("row", "col"),
        P("row", "col"),
        P("col", "row"),
    )
    out_specs = (
        P(("group", "col"), "row"),
        P(("group", "col"), "row"),
        P(("group", "row"), "col"),
        P(("group", "row"), "col"),
        P(("group", "col"), "row"),
    )
    step = functools.partial(body, mesh.shape["col"] == 8)
    return jax.shard_map(step, mesh=mesh, in_specs=in_specs, out_specs=out_specs, check_vma=False)
```
